32 devices in a mesh: group: 2 (over y), expert: 8 (over z, x), tensor: 2 (over core).
Axes of the slice: x: 2, y: 2, z: 4, core: 2. Of those that a mesh axis runs over, the one named last changes fastest.
Arguments:
- tokens: bfloat16 [64, 5120], P(('group', 'expert'), 'tensor'), parts along dimension 0, may hold values from -6 to 6
- expert_ids: int32 [64, 1], P(('group', 'expert')), parts along dimension 0, may hold values from 0 to 3; in each aligned block of 4 rows (0 to 3, 4 to 7, ...) at most 2 rows name the same one
- route_scale: float32 [64], P(('group', 'expert')), parts along dimension 0, may hold values from 0.1 to 1
- gate_weight: bfloat16 [8, 5120, 4096], P('expert', None, 'tensor'), may hold values from -0.078125 to 0.078125
- up_weight: bfloat16 [8, 5120, 4096], P('expert', None, 'tensor'), may hold values from -0.078125 to 0.078125
- down_weight: bfloat16 [8, 4096, 5120], P('expert', 'tensor'), may hold values from -0.0625 to 0.0625
Outputs:
- routed: bfloat16 [64, 5120], P(('group', 'expert'), 'tensor'), parts along dimension 0
The draws below stay inside these ranges and needn't reach their ends.
There are 2 independent parts, one for each index of `group`. The reference program is written for one: setup_inputs(seed, part) draws one part's arguments, and reference() takes and returns one part's arrays. A program takes and returns all parts, laid end to end along the dimension named above; an argument that names none is the same for every part. Nothing has to cross between parts.
Inputs may be any that keep to these rules, and one draw needn't show every extreme that they name: `expert_ids`: ids of experts 0 to 3. In each aligned block of 4 rows (the rows of one index of the expert axis) no expert is named by more than 2 rows, a bound that some block reaches.
All inputs are finite; a program needn't handle non-finite values.
Results may differ from the reference program's by a relative error of at most 0.0051.
Values may be sent and summed in bfloat16 or wider, within the bound.
A program may use at most 192 MiB of HBM per device.

```python
import math
import jax
import jax.numpy as jnp
import numpy as np

D = 5120
FF = 8192
TOK_DEV = 4
NE = 4
CAP = 2
TOKENS = 32
FF_SLAB = 4096
N_EXPERT = 8


def steps_of(rng, dims, pieces, low, top_value):
    def one(dim, parts):
        steps = jax.random.uniform(jax.random.fold_in(jax.random.fold_in(rng, 6), dim), (parts,), jnp.float32, low / len(pieces), top_value / len(pieces))
        return jnp.repeat(jnp.exp(steps), dims[dim] // parts).reshape((-1,) + (1,) * (len(dims) - dim - 1))

    factor_of = one(*pieces[0])
    for cut in pieces[1:]:
        factor_of = factor_of * one(*cut)
    return factor_of


def routed_block(own_key, own, number, rows, amount, top, most, slope):
    ranking = jax.random.permutation(own_key, amount)
    heavy_load, common = portions_of(amount, rows * top, most, slope, True), portions_of(amount, rows * top, most, slope, False)
    places = jnp.arange(amount)

    def named(sizes, turn):
        used = int((sizes > 0).sum())
        fixed = max(1, used // 4)
        shifted = fixed + (places - fixed + turn * (used - fixed)) % max(1, amount - fixed)
        return jnp.zeros((amount,), jnp.int32).at[ranking[jnp.where(places < fixed, places, shifted)]].set(jnp.asarray(sizes, jnp.int32))

    sizes = jnp.where(number % 4 == 0, named(heavy_load, number // 4), named(common, number - number // 4 - 1))
    mixed = jax.random.permutation(jax.random.fold_in(own, 3), amount)
    source_of, taker = mixed[0:amount // 2 * 2:2], mixed[1:amount // 2 * 2:2]
    room = jnp.minimum(sizes[source_of] - 1, most - sizes[taker]) // 2
    room = jnp.where((source_of == ranking[0]) | (taker == ranking[0]) | (sizes[taker] == 0), 0, jnp.maximum(room, 0))
    shifted = jax.random.randint(jax.random.fold_in(own, 4), (amount // 2,), 0, 1 << 20) % (room + 1)
    sizes = sizes.at[source_of].add(-shifted).at[taker].add(shifted)
    labels = jnp.searchsorted(jnp.cumsum(sizes), jnp.arange(rows * top), side="right").astype(jnp.int32)
    grid = labels.reshape(top, rows).T
    grid = grid[jax.random.permutation(jax.random.fold_in(own, 1), rows)]
    turn = jax.random.randint(jax.random.fold_in(own, 2), (rows, 1), 0, top)
    return jnp.take_along_axis(grid, (jnp.arange(top)[None, :] + turn) % top, axis=1)


def portions_of(amount, total, most, skew, full):
    loads = [(1 << 20) // math.isqrt(grade ** skew) + 1 for grade in range(1, amount + 1)]
    largest = most if full else min(most, max(-(-total // amount), total * loads[0] // sum(loads)))
    least = 1 if total - largest >= amount - 1 else 0
    given, surplus = [largest] + [least] * (amount - 1), total - largest - least * (amount - 1)
    while surplus > 0:
        movable = [i for i in range(1, amount) if given[i] < largest] or [i for i in range(1, amount) if given[i] < most]
        pool, budget = sum([loads[i] for i in movable]), surplus
        for i in movable:
            more = min(most - given[i], max(1, budget * loads[i] // pool), surplus)
            given[i] = given[i] + more
            surplus = surplus - more
    return np.array(given)


def centred(key, extent, scale, reach, cuts=(), kind=jnp.bfloat16):
    values = scale * jax.random.normal(key, extent, jnp.float32)
    if cuts:
        values = values * steps_of(key, extent, cuts, -0.22, 0.18)
    return jnp.clip(values, -reach, reach).astype(kind)


def setup_inputs(seed: int = 0, part: int = 0) -> dict:
    seeds = jax.random.split(jax.random.key(seed), 7)
    part_keys = jax.random.split(jax.random.fold_in(seeds[6], part), 7)
    tokens = centred(part_keys[0], (TOKENS, D), 1.0, 6.0, ((0, 8), (1, 2)))
    expert_ids_keys = jax.random.split(jax.random.fold_in(part_keys[1], 1), TOKENS // TOK_DEV)
    expert_ids_turns = jax.random.permutation(jax.random.fold_in(part_keys[1], 3), TOKENS // TOK_DEV)
    expert_ids = jax.vmap(lambda own, number: routed_block(jax.random.fold_in(part_keys[1], 2), own, number, TOK_DEV, NE, 1, CAP, 2))(expert_ids_keys, expert_ids_turns).reshape((TOKENS, 1))
    route_scale = jnp.clip(0.1 + 0.9 * jax.random.uniform(part_keys[2], (TOKENS,), jnp.float32) ** steps_of(part_keys[2], (TOKENS,), ((0, 8),), -0.2, 0.2), 0.1, 1.0)
    gate_weight = centred(seeds[3], (N_EXPERT, D, FF_SLAB), D ** -0.5, 0.078125, ((0, 8), (2, 2)))
    up_weight = centred(seeds[4], (N_EXPERT, D, FF_SLAB), D ** -0.5, 0.078125, ((0, 8), (2, 2)))
    down_weight = centred(seeds[5], (N_EXPERT, FF_SLAB, D), FF ** -0.5, 0.0625, ((0, 8), (1, 2)))
    return dict(tokens=tokens, expert_ids=expert_ids, route_scale=route_scale, gate_weight=gate_weight, up_weight=up_weight, down_weight=down_weight)


def reference(tokens, expert_ids, route_scale, gate_weight, up_weight, down_weight):
    per_expert = N_EXPERT // NE
    limit = N_EXPERT * CAP
    ids = expert_ids[:, 0]
    routed = jnp.zeros((TOKENS, D), jnp.float32)
    for expert in range(NE):
        order = jnp.argsort((ids != expert).astype(jnp.int32), stable=True)[:limit].astype(jnp.int32)
        rows = tokens[order]
        low = expert * per_expert
        high = low + per_expert
        w_gate = gate_weight[low:high].transpose(1, 0, 2).reshape(D, FF)
        w_up = up_weight[low:high].transpose(1, 0, 2).reshape(D, FF)
        w_down = down_weight[low:high].reshape(FF, D)
        gate = jnp.dot(rows, w_gate, preferred_element_type=jnp.float32)
        up_part = jnp.dot(rows, w_up, preferred_element_type=jnp.float32)
        hidden = (jax.nn.silu(gate) * up_part).astype(jnp.bfloat16)
        result = jnp.dot(hidden, w_down, preferred_element_type=jnp.float32)
        keep = (ids[order] == expert)[:, None]
        routed = routed.at[order].add(jnp.where(keep, result, jnp.float32(0.0)))
    return (routed * route_scale[:, None]).astype(jnp.bfloat16)
```

```python
import functools

import jax
import jax.numpy as jnp
from jax import lax
from jax.experimental import pallas as pl
from jax.experimental.pallas import tpu as pltpu
from jax.sharding import PartitionSpec as P

NE = 4
CAP = 2
MESH = pl.DeviceIdType.MESH
F32 = jnp.float32
BF16 = jnp.bfloat16


def chunk_of(size):
    for width in (512, 256, 128):
        if size % width == 0:
            return width
    return size


def groups_of(count):
    first = (count + 1) // 2
    return [g for g in (first, count - first) if g]


def each(count, body):
    for i in range(count):
        body(i)


def kernel(
    n, ids_ref, scale_ref, tok_ref, gate_ref, up_ref, down_ref, out_ref,
    w_gate, w_up, w_down, placed, snd, recv, rows32, flat_own, flat_other,
    acc_gate, acc_up, hidden, cross_out, cross_in, part32, summed, osnd0, orecv0, osnd1, orecv1,
    gate_sem, up_sem, down_sem, snd_sem, recv_sem, flat_sem, cross_ssem, cross_rsem, out_ssem, out_rsem,
):
    me = lax.axis_index("expert")
    core = lax.axis_index("tensor")
    other = 1 - core
    per = n // NE
    tok_rows, half = tok_ref.shape
    chunk = flat_own.shape[2]
    nc = half // chunk
    groups = groups_of(nc)
    osnd, orecv = (osnd0, osnd1), (orecv0, orecv1)

    def peer(d):
        return lax.rem(me + d, n)

    barrier = pltpu.get_barrier_semaphore()
    pl.semaphore_signal(barrier, inc=1, device_id={"tensor": other}, device_id_type=MESH)

    @pl.loop(1, n)
    def _(d):
        pl.semaphore_signal(barrier, inc=1, device_id={"expert": peer(d)}, device_id_type=MESH)

    def row_of(c):
        side = jnp.where(c < nc, core, other)
        return pl.multiple_of((side * nc + lax.rem(c, nc)) * chunk, chunk)

    def col_of(c):
        side = jnp.where(c < nc, other, core)
        return pl.multiple_of((side * nc + lax.rem(c, nc)) * chunk, chunk)

    def gate_copy(c):
        return pltpu.make_async_copy(gate_ref.at[0, pl.ds(row_of(c), chunk), :], w_gate.at[c], gate_sem.at[c])

    def up_copy(c):
        return pltpu.make_async_copy(up_ref.at[0, pl.ds(row_of(c), chunk), :], w_up.at[c], up_sem.at[c])

    def down_copy(c):
        return pltpu.make_async_copy(down_ref.at[0, :, pl.ds(col_of(c), chunk)], w_down.at[c], down_sem.at[c])

    @pl.loop(0, 2 * nc)
    def _(c):
        gate_copy(c).start()
        up_copy(c).start()

    ids = [ids_ref[i, 0] for i in range(tok_rows)]
    keys = []
    for i in range(tok_rows):
        slot = jnp.int32(0)
        for j in range(i):
            slot = slot + (ids[j] == ids[i]).astype(jnp.int32)
        keys.append(ids[i] * CAP + slot)
    tok = tok_ref[...].astype(F32)
    slots = lax.broadcasted_iota(jnp.int32, (NE * CAP, 1), 0)
    total = jnp.zeros((NE * CAP, half), F32)
    for i in range(tok_rows):
        total = total + jnp.where(slots == keys[i], 1.0, 0.0).astype(F32) * tok[i : i + 1, :]
    placed[...] = total
    for e in range(NE):
        snd[e] = placed[e * CAP : (e + 1) * CAP, :].astype(BF16)

    pl.semaphore_wait(barrier, n)

    def send_copy(d):
        to = peer(d)
        return pltpu.make_async_remote_copy(
            src_ref=snd.at[to // per], dst_ref=recv.at[me], send_sem=snd_sem.at[d], recv_sem=recv_sem.at[me],
            device_id={"expert": to}, device_id_type=MESH,
        )

    def recv_copy(d):
        source = peer(d)
        return pltpu.make_async_remote_copy(
            src_ref=snd.at[0], dst_ref=recv.at[source], send_sem=snd_sem.at[d], recv_sem=recv_sem.at[source],
            device_id={"expert": source}, device_id_type=MESH,
        )

    @pl.loop(1, n)
    def _(d):
        send_copy(d).start()

    @pl.loop(0, 2 * nc)
    def _(c):
        down_copy(c).start()

    recv[me] = snd[me // per]

    @pl.loop(1, n)
    def _(d):
        recv_copy(d).wait_recv()

    def unpack(i):
        rows32[pl.ds(i * CAP, CAP), :] = recv[i].astype(F32)

    each(n, unpack)
    for c in range(nc):
        flat_own[c] = rows32[:, c * chunk : (c + 1) * chunk].astype(BF16)
    flat_copy = pltpu.make_async_remote_copy(
        src_ref=flat_own, dst_ref=flat_other, send_sem=flat_sem.at[0], recv_sem=flat_sem.at[1],
        device_id={"tensor": other}, device_id_type=MESH,
    )
    flat_copy.start()

    acc_gate[...] = jnp.zeros_like(acc_gate)
    acc_up[...] = jnp.zeros_like(acc_up)

    def gate_up(flat, base):
        @pl.loop(0, nc)
        def _(c):
            lhs = flat[c]
            gate_copy(base + c).wait()
            acc_gate[...] += jnp.dot(lhs, w_gate[base + c], preferred_element_type=F32)
            up_copy(base + c).wait()
            acc_up[...] += jnp.dot(lhs, w_up[base + c], preferred_element_type=F32)

    gate_up(flat_own, 0)
    flat_copy.wait_recv()
    gate_up(flat_other, nc)
    value = acc_gate[...]
    hidden[...] = (value / (1.0 + jnp.exp(-value)) * acc_up[...]).astype(BF16)

    def cross_copy(c):
        return pltpu.make_async_remote_copy(
            src_ref=cross_out.at[c], dst_ref=cross_in.at[c], send_sem=cross_ssem.at[c], recv_sem=cross_rsem.at[c],
            device_id={"tensor": other}, device_id_type=MESH,
        )

    @pl.loop(0, nc)
    def _(c):
        down_copy(c).wait()
        cross_out[c] = jnp.dot(hidden[...], w_down[c], preferred_element_type=F32)
        cross_copy(c).start()

    def out_copy(g, d, source):
        to = peer(d)
        row = to if source else me
        return pltpu.make_async_remote_copy(
            src_ref=osnd[g].at[to], dst_ref=orecv[g].at[row],
            send_sem=out_ssem.at[g, d], recv_sem=out_rsem.at[g, row],
            device_id={"expert": to}, device_id_type=MESH,
        )

    first = 0
    for g, count in enumerate(groups):
        for c in range(count):
            at = nc + first + c
            down_copy(at).wait()
            result = jnp.dot(hidden[...], w_down[at], preferred_element_type=F32)
            cross_copy(first + c).wait_recv()
            part32[:, c * chunk : (c + 1) * chunk] = result + cross_in[first + c]

        def pack(i, g=g, count=count):
            osnd[g][i] = part32[pl.ds(i * CAP, CAP), : count * chunk].astype(BF16)

        each(n, pack)

        @pl.loop(1, n)
        def _(d, g=g):
            out_copy(g, d, False).start()

        orecv[g][me] = osnd[g][me]
        first += count

    lanes = lax.broadcasted_iota(jnp.int32, (tok_rows, 1), 0)
    key = jnp.zeros((tok_rows, 1), jnp.int32)
    scale = jnp.zeros((tok_rows, 1), F32)
    for i in range(tok_rows):
        key = jnp.where(lanes == i, keys[i], key)
        scale = jnp.where(lanes == i, scale_ref[i], scale)
    first = 0
    for g, count in enumerate(groups):

        @pl.loop(1, n)
        def _(d, g=g):
            out_copy(g, d, True).wait_recv()

        width = count * chunk
        for e in range(NE):
            if per <= 8:
                rows = orecv[g][e * per].astype(F32)
                for j in range(1, per):
                    rows = rows + orecv[g][e * per + j].astype(F32)
                summed[e * CAP : (e + 1) * CAP, :width] = rows
            else:
                summed[e * CAP : (e + 1) * CAP, :width] = jnp.zeros((CAP, width), F32)

                @pl.loop(0, per)
                def _(j, g=g, e=e, width=width):
                    summed[e * CAP : (e + 1) * CAP, :width] += orecv[g][e * per + j].astype(F32)

        mine = jnp.zeros((tok_rows, width), F32)
        for r in range(NE * CAP):
            mine = mine + jnp.where(key == r, 1.0, 0.0).astype(F32) * summed[r : r + 1, :width]
        out_ref[:, first * chunk : first * chunk + width] = (mine * scale).astype(BF16)
        first += count

    flat_copy.wait_send()

    @pl.loop(1, n)
    def _(d):
        send_copy(d).wait_send()

    @pl.loop(0, nc)
    def _(c):
        cross_copy(c).wait_send()

    for g in range(len(groups)):

        @pl.loop(1, n)
        def _(d, g=g):
            out_copy(g, d, False).wait_send()


def local(tokens, expert_ids, route_scale, gate_weight, up_weight, down_weight):
    n = lax.axis_size("expert")
    tok_rows, half = tokens.shape
    width = gate_weight.shape[2]
    rows = n * CAP
    chunk = chunk_of(half)
    nc = half // chunk
    groups = groups_of(nc)
    sizes = [g * chunk for g in groups]
    if len(sizes) == 1:
        sizes = sizes + sizes
    dma = pltpu.SemaphoreType.DMA
    vmem = pl.BlockSpec(memory_space=pltpu.VMEM)
    smem = pl.BlockSpec(memory_space=pltpu.SMEM)
    hbm = pl.BlockSpec(memory_space=pl.ANY)
    return pl.pallas_call(
        functools.partial(kernel, n),
        out_shape=jax.ShapeDtypeStruct((tok_rows, half), BF16),
        in_specs=[smem, smem, vmem, hbm, hbm, hbm],
        out_specs=vmem,
        scratch_shapes=[
            pltpu.VMEM((2 * nc, chunk, width), BF16),
            pltpu.VMEM((2 * nc, chunk, width), BF16),
            pltpu.VMEM((2 * nc, width, chunk), BF16),
            pltpu.VMEM((NE * CAP, half), F32),
            pltpu.VMEM((NE, CAP, half), BF16),
            pltpu.VMEM((n, CAP, half), BF16),
            pltpu.VMEM((rows, half), F32),
            pltpu.VMEM((nc, rows, chunk), BF16),
            pltpu.VMEM((nc, rows, chunk), BF16),
            pltpu.VMEM((rows, width), F32),
            pltpu.VMEM((rows, width), F32),
            pltpu.VMEM((rows, width), BF16),
            pltpu.VMEM((nc, rows, chunk), F32),
            pltpu.VMEM((nc, rows, chunk), F32),
            pltpu.VMEM((rows, sizes[0]), F32),
            pltpu.VMEM((NE * CAP, sizes[0]), F32),
            pltpu.VMEM((n, CAP, sizes[0]), BF16),
            pltpu.VMEM((n, CAP, sizes[0]), BF16),
            pltpu.VMEM((n, CAP, sizes[1]), BF16),
            pltpu.VMEM((n, CAP, sizes[1]), BF16),
            dma((2 * nc,)),
            dma((2 * nc,)),
            dma((2 * nc,)),
            dma((n,)),
            dma((n,)),
            dma((2,)),
            dma((nc,)),
            dma((nc,)),
            dma((2, n)),
            dma((2, n)),
        ],
        compiler_params=pltpu.CompilerParams(
            collective_id=0, has_side_effects=True, vmem_limit_bytes=66_900_000
        ),
        cost_estimate=pl.CostEstimate(
            flops=6 * rows * 2 * half * width, bytes_accessed=12 * half * width, transcendentals=rows * width
        ),
    )(expert_ids, route_scale, tokens, gate_weight, up_weight, down_weight)


def solution(mesh):
    in_specs = (
        P(("group", "expert"), "tensor"),
        P(("group", "expert"), None),
        P(("group", "expert")),
        P("expert", None, "tensor"),
        P("expert", None, "tensor"),
        P("expert", "tensor", None),
    )
    out_specs = P(("group", "expert"), "tensor")
    return jax.shard_map(local, mesh=mesh, in_specs=in_specs, out_specs=out_specs, check_vma=False)
```

```python
import functools

import jax
import jax.numpy as jnp
from jax import lax
from jax.experimental import pallas as pl
from jax.experimental.pallas import tpu as pltpu
from jax.sharding import PartitionSpec as P

NE = 4
CAP = 2
MESH = pl.DeviceIdType.MESH
F32 = jnp.float32
BF16 = jnp.bfloat16


def chunk_of(size):
    for width in (512, 256, 128):
        if size % width == 0:
            return width
    return size


def groups_of(count):
    first = (count + 1) // 2
    return [g for g in (first, count - first) if g]


def each(count, body):
    for i in range(count):
        body(i)


def kernel(
    n, ids_ref, tok_ref, gate_ref, up_ref, down_ref, out_ref,
    w_gate, w_up, w_down, placed, snd, recv, rows32, flat_own, flat_other,
    acc_gate, acc_up, hidden, cross_out, cross_in, part32, summed, osnd0, orecv0, osnd1, orecv1,
    gate_sem, up_sem, down_sem, snd_sem, recv_sem, flat_sem, cross_ssem, cross_rsem, out_ssem, out_rsem,
):
    me = lax.axis_index("expert")
    core = lax.axis_index("tensor")
    other = 1 - core
    per = n // NE
    tok_rows, half = tok_ref.shape
    chunk = flat_own.shape[2]
    nc = half // chunk
    groups = groups_of(nc)
    osnd, orecv = (osnd0, osnd1), (orecv0, orecv1)

    def peer(d):
        return lax.rem(me + d, n)

    barrier = pltpu.get_barrier_semaphore()
    pl.semaphore_signal(barrier, inc=1, device_id={"tensor": other}, device_id_type=MESH)

    @pl.loop(1, n)
    def _(d):
        pl.semaphore_signal(barrier, inc=1, device_id={"expert": peer(d)}, device_id_type=MESH)

    def row_of(c):
        side = jnp.where(c < nc, core, other)
        return pl.multiple_of((side * nc + lax.rem(c, nc)) * chunk, chunk)

    def col_of(c):
        side = jnp.where(c < nc, other, core)
        return pl.multiple_of((side * nc + lax.rem(c, nc)) * chunk, chunk)

    def gate_copy(c):
        return pltpu.make_async_copy(gate_ref.at[0, pl.ds(row_of(c), chunk), :], w_gate.at[c], gate_sem.at[c])

    def up_copy(c):
        return pltpu.make_async_copy(up_ref.at[0, pl.ds(row_of(c), chunk), :], w_up.at[c], up_sem.at[c])

    def down_copy(c):
        return pltpu.make_async_copy(down_ref.at[0, :, pl.ds(col_of(c), chunk)], w_down.at[c], down_sem.at[c])

    @pl.loop(0, 2 * nc)
    def _(c):
        gate_copy(c).start()
        up_copy(c).start()

    ids = [ids_ref[i] for i in range(tok_rows)]
    keys = []
    for i in range(tok_rows):
        slot = jnp.int32(0)
        for j in range(i):
            slot = slot + (ids[j] == ids[i]).astype(jnp.int32)
        keys.append(ids[i] * CAP + slot)
    tok = tok_ref[...].astype(F32)
    slots = lax.broadcasted_iota(jnp.int32, (NE * CAP, 1), 0)
    total = jnp.zeros((NE * CAP, half), F32)
    for i in range(tok_rows):
        total = total + jnp.where(slots == keys[i], 1.0, 0.0).astype(F32) * tok[i : i + 1, :]
    placed[...] = total
    for e in range(NE):
        snd[e] = placed[e * CAP : (e + 1) * CAP, :].astype(BF16)

    pl.semaphore_wait(barrier, n)

    def send_copy(d):
        to = peer(d)
        return pltpu.make_async_remote_copy(
            src_ref=snd.at[to // per], dst_ref=recv.at[me], send_sem=snd_sem.at[d], recv_sem=recv_sem.at[me],
            device_id={"expert": to}, device_id_type=MESH,
        )

    def recv_copy(d):
        source = peer(d)
        return pltpu.make_async_remote_copy(
            src_ref=snd.at[0], dst_ref=recv.at[source], send_sem=snd_sem.at[d], recv_sem=recv_sem.at[source],
            device_id={"expert": source}, device_id_type=MESH,
        )

    @pl.loop(1, n)
    def _(d):
        send_copy(d).start()

    @pl.loop(0, 2 * nc)
    def _(c):
        down_copy(c).start()

    recv[me] = snd[me // per]

    @pl.loop(1, n)
    def _(d):
        recv_copy(d).wait_recv()

    def unpack(i):
        rows32[pl.ds(i * CAP, CAP), :] = recv[i].astype(F32)

    each(n, unpack)
    for c in range(nc):
        flat_own[c] = rows32[:, c * chunk : (c + 1) * chunk].astype(BF16)
    flat_copy = pltpu.make_async_remote_copy(
        src_ref=flat_own, dst_ref=flat_other, send_sem=flat_sem.at[0], recv_sem=flat_sem.at[1],
        device_id={"tensor": other}, device_id_type=MESH,
    )
    flat_copy.start()

    acc_gate[...] = jnp.zeros_like(acc_gate)
    acc_up[...] = jnp.zeros_like(acc_up)

    def gate_up(flat, base):
        @pl.loop(0, nc)
        def _(c):
            lhs = flat[c]
            gate_copy(base + c).wait()
            acc_gate[...] += jnp.dot(lhs, w_gate[base + c], preferred_element_type=F32)
            up_copy(base + c).wait()
            acc_up[...] += jnp.dot(lhs, w_up[base + c], preferred_element_type=F32)

    gate_up(flat_own, 0)
    flat_copy.wait_recv()
    gate_up(flat_other, nc)
    value = acc_gate[...]
    hidden[...] = (value / (1.0 + jnp.exp(-value)) * acc_up[...]).astype(BF16)

    def cross_copy(c):
        return pltpu.make_async_remote_copy(
            src_ref=cross_out.at[c], dst_ref=cross_in.at[c], send_sem=cross_ssem.at[c], recv_sem=cross_rsem.at[c],
            device_id={"tensor": other}, device_id_type=MESH,
        )

    @pl.loop(0, nc)
    def _(c):
        down_copy(c).wait()
        cross_out[c] = jnp.dot(hidden[...], w_down[c], preferred_element_type=F32)
        cross_copy(c).start()

    def out_copy(g, d, source):
        to = peer(d)
        row = to if source else me
        return pltpu.make_async_remote_copy(
            src_ref=osnd[g].at[to], dst_ref=orecv[g].at[row],
            send_sem=out_ssem.at[g, d], recv_sem=out_rsem.at[g, row],
            device_id={"expert": to}, device_id_type=MESH,
        )

    first = 0
    for g, count in enumerate(groups):
        for c in range(count):
            at = nc + first + c
            down_copy(at).wait()
            result = jnp.dot(hidden[...], w_down[at], preferred_element_type=F32)
            cross_copy(first + c).wait_recv()
            part32[:, c * chunk : (c + 1) * chunk] = result + cross_in[first + c]

        def pack(i, g=g, count=count):
            osnd[g][i] = part32[pl.ds(i * CAP, CAP), : count * chunk].astype(BF16)

        each(n, pack)

        @pl.loop(1, n)
        def _(d, g=g):
            out_copy(g, d, False).start()

        orecv[g][me] = osnd[g][me]
        first += count

    lanes = lax.broadcasted_iota(jnp.int32, (tok_rows, 1), 0)
    key = jnp.zeros((tok_rows, 1), jnp.int32)
    for i in range(tok_rows):
        key = jnp.where(lanes == i, keys[i], key)
    first = 0
    for g, count in enumerate(groups):

        @pl.loop(1, n)
        def _(d, g=g):
            out_copy(g, d, True).wait_recv()

        width = count * chunk
        for e in range(NE):
            if per <= 8:
                rows = orecv[g][e * per].astype(F32)
                for j in range(1, per):
                    rows = rows + orecv[g][e * per + j].astype(F32)
                summed[e * CAP : (e + 1) * CAP, :width] = rows
            else:
                summed[e * CAP : (e + 1) * CAP, :width] = jnp.zeros((CAP, width), F32)

                @pl.loop(0, per)
                def _(j, g=g, e=e, width=width):
                    summed[e * CAP : (e + 1) * CAP, :width] += orecv[g][e * per + j].astype(F32)

        mine = jnp.zeros((tok_rows, width), F32)
        for r in range(NE * CAP):
            mine = mine + jnp.where(key == r, 1.0, 0.0).astype(F32) * summed[r : r + 1, :width]
        out_ref[:, first * chunk : first * chunk + width] = mine
        first += count

    flat_copy.wait_send()

    @pl.loop(1, n)
    def _(d):
        send_copy(d).wait_send()

    @pl.loop(0, nc)
    def _(c):
        cross_copy(c).wait_send()

    for g in range(len(groups)):

        @pl.loop(1, n)
        def _(d, g=g):
            out_copy(g, d, False).wait_send()


def local(tokens, expert_ids, route_scale, gate_weight, up_weight, down_weight):
    n = lax.axis_size("expert")
    tok_rows, half = tokens.shape
    width = gate_weight.shape[2]
    rows = n * CAP
    chunk = chunk_of(half)
    nc = half // chunk
    groups = groups_of(nc)
    sizes = [g * chunk for g in groups]
    if len(sizes) == 1:
        sizes = sizes + sizes
    dma = pltpu.SemaphoreType.DMA
    vmem = pl.BlockSpec(memory_space=pltpu.VMEM)
    smem = pl.BlockSpec(memory_space=pltpu.SMEM)
    hbm = pl.BlockSpec(memory_space=pl.ANY)
    summed = pl.pallas_call(
        functools.partial(kernel, n),
        out_shape=jax.ShapeDtypeStruct((tok_rows, half), F32),
        in_specs=[smem, vmem, hbm, hbm, hbm],
        out_specs=vmem,
        scratch_shapes=[
            pltpu.VMEM((2 * nc, chunk, width), BF16),
            pltpu.VMEM((2 * nc, chunk, width), BF16),
            pltpu.VMEM((2 * nc, width, chunk), BF16),
            pltpu.VMEM((NE * CAP, half), F32),
            pltpu.VMEM((NE, CAP, half), BF16),
            pltpu.VMEM((n, CAP, half), BF16),
            pltpu.VMEM((rows, half), F32),
            pltpu.VMEM((nc, rows, chunk), BF16),
            pltpu.VMEM((nc, rows, chunk), BF16),
            pltpu.VMEM((rows, width), F32),
            pltpu.VMEM((rows, width), F32),
            pltpu.VMEM((rows, width), BF16),
            pltpu.VMEM((nc, rows, chunk), F32),
            pltpu.VMEM((nc, rows, chunk), F32),
            pltpu.VMEM((rows, sizes[0]), F32),
            pltpu.VMEM((NE * CAP, sizes[0]), F32),
            pltpu.VMEM((n, CAP, sizes[0]), BF16),
            pltpu.VMEM((n, CAP, sizes[0]), BF16),
            pltpu.VMEM((n, CAP, sizes[1]), BF16),
            pltpu.VMEM((n, CAP, sizes[1]), BF16),
            dma((2 * nc,)),
            dma((2 * nc,)),
            dma((2 * nc,)),
            dma((n,)),
            dma((n,)),
            dma((2,)),
            dma((nc,)),
            dma((nc,)),
            dma((2, n)),
            dma((2, n)),
        ],
        compiler_params=pltpu.CompilerParams(
            collective_id=0, has_side_effects=True, vmem_limit_bytes=66_900_000
        ),
        cost_estimate=pl.CostEstimate(
            flops=6 * rows * 2 * half * width, bytes_accessed=12 * half * width, transcendentals=rows * width
        ),
    )(expert_ids.reshape(tok_rows), tokens, gate_weight, up_weight, down_weight)
    return (summed * route_scale[:, None]).astype(BF16)


def solution(mesh):
    in_specs = (
        P(("group", "expert"), "tensor"),
        P(("group", "expert"), None),
        P(("group", "expert")),
        P("expert", None, "tensor"),
        P("expert", None, "tensor"),
        P("expert", "tensor", None),
    )
    out_specs = P(("group", "expert"), "tensor")
    return jax.shard_map(local, mesh=mesh, in_specs=in_specs, out_specs=out_specs, check_vma=False)
```

```python
import functools

import jax
import jax.numpy as jnp
from jax import lax
from jax.experimental import pallas as pl
from jax.experimental.pallas import tpu as pltpu
from jax.sharding import PartitionSpec as P

NE = 4
CAP = 2
MESH = pl.DeviceIdType.MESH
F32 = jnp.float32
BF16 = jnp.bfloat16


def chunk_of(size):
    for width in (512, 256, 128):
        if size % width == 0:
            return width
    return size


def groups_of(count):
    first = max(count - 1, 1)
    return [g for g in (first, count - first) if g]


def each(count, body):
    for i in range(count):
        body(i)


def kernel(
    n, ids_ref, tok_ref, gate_ref, up_ref, down_ref, out_ref,
    w_gate, w_up, w_down, placed, snd, recv, rows32, flat_own, flat_other,
    acc_gate, acc_up, hidden, cross_out, cross_in, part32, summed, osnd0, orecv0, osnd1, orecv1,
    gate_sem, up_sem, down_sem, snd_sem, recv_sem, flat_sem, cross_ssem, cross_rsem, out_ssem, out_rsem,
):
    me = lax.axis_index("expert")
    core = lax.axis_index("tensor")
    other = 1 - core
    per = n // NE
    tok_rows, half = tok_ref.shape
    chunk = flat_own.shape[2]
    nc = half // chunk
    groups = groups_of(nc)
    osnd, orecv = (osnd0, osnd1), (orecv0, orecv1)

    def peer(d):
        return lax.rem(me + d, n)

    def row_of(c):
        side = jnp.where(c < nc, core, other)
        return pl.multiple_of((side * nc + lax.rem(c, nc)) * chunk, chunk)

    def col_of(c):
        side = jnp.where(c < nc, other, core)
        return pl.multiple_of((side * nc + lax.rem(c, nc)) * chunk, chunk)

    def gate_copy(c):
        return pltpu.make_async_copy(gate_ref.at[0, pl.ds(row_of(c), chunk), :], w_gate.at[c], gate_sem.at[c])

    def up_copy(c):
        return pltpu.make_async_copy(up_ref.at[0, pl.ds(row_of(c), chunk), :], w_up.at[c], up_sem.at[c])

    def down_copy(c):
        return pltpu.make_async_copy(down_ref.at[0, :, pl.ds(col_of(c), chunk)], w_down.at[c], down_sem.at[c])

    for c in range(2):
        gate_copy(c).start()
        up_copy(c).start()

    barrier = pltpu.get_barrier_semaphore()
    pl.semaphore_signal(barrier, inc=1, device_id={"tensor": other}, device_id_type=MESH)

    @pl.loop(1, n)
    def _(d):
        pl.semaphore_signal(barrier, inc=1, device_id={"expert": peer(d)}, device_id_type=MESH)

    @pl.loop(2, 2 * nc)
    def _(c):
        gate_copy(c).start()
        up_copy(c).start()

    ids = [ids_ref[i] for i in range(tok_rows)]
    keys = []
    for i in range(tok_rows):
        slot = jnp.int32(0)
        for j in range(i):
            slot = slot + (ids[j] == ids[i]).astype(jnp.int32)
        keys.append(ids[i] * CAP + slot)
    tok = tok_ref[...].astype(F32)
    slots = lax.broadcasted_iota(jnp.int32, (NE * CAP, 1), 0)
    total = jnp.zeros((NE * CAP, half), F32)
    for i in range(tok_rows):
        total = total + jnp.where(slots == keys[i], 1.0, 0.0).astype(F32) * tok[i : i + 1, :]
    placed[...] = total
    for e in range(NE):
        snd[e] = placed[e * CAP : (e + 1) * CAP, :].astype(BF16)

    pl.semaphore_wait(barrier, n)

    def send_copy(d):
        to = peer(d)
        return pltpu.make_async_remote_copy(
            src_ref=snd.at[to // per], dst_ref=recv.at[me], send_sem=snd_sem.at[d], recv_sem=recv_sem.at[me],
            device_id={"expert": to}, device_id_type=MESH,
        )

    def recv_copy(d):
        source = peer(d)
        return pltpu.make_async_remote_copy(
            src_ref=snd.at[0], dst_ref=recv.at[source], send_sem=snd_sem.at[d], recv_sem=recv_sem.at[source],
            device_id={"expert": source}, device_id_type=MESH,
        )

    @pl.loop(1, n)
    def _(d):
        send_copy(d).start()

    @pl.loop(0, 2 * nc)
    def _(c):
        down_copy(c).start()

    recv[me] = snd[me // per]

    @pl.loop(1, n)
    def _(d):
        recv_copy(d).wait_recv()

    def unpack(i):
        rows32[pl.ds(i * CAP, CAP), :] = recv[i].astype(F32)

    each(n, unpack)
    for c in range(nc):
        flat_own[c] = rows32[:, c * chunk : (c + 1) * chunk].astype(BF16)
    flat_copy = pltpu.make_async_remote_copy(
        src_ref=flat_own, dst_ref=flat_other, send_sem=flat_sem.at[0], recv_sem=flat_sem.at[1],
        device_id={"tensor": other}, device_id_type=MESH,
    )
    flat_copy.start()

    acc_gate[...] = jnp.zeros_like(acc_gate)
    acc_up[...] = jnp.zeros_like(acc_up)

    def gate_up(flat, base):
        @pl.loop(0, nc)
        def _(c):
            lhs = flat[c]
            gate_copy(base + c).wait()
            acc_gate[...] += jnp.dot(lhs, w_gate[base + c], preferred_element_type=F32)
            up_copy(base + c).wait()
            acc_up[...] += jnp.dot(lhs, w_up[base + c], preferred_element_type=F32)

    gate_up(flat_own, 0)
    flat_copy.wait_recv()
    gate_up(flat_other, nc)
    value = acc_gate[...]
    hidden[...] = (value / (1.0 + jnp.exp(-value)) * acc_up[...]).astype(BF16)

    def cross_copy(c):
        return pltpu.make_async_remote_copy(
            src_ref=cross_out.at[c], dst_ref=cross_in.at[c], send_sem=cross_ssem.at[c], recv_sem=cross_rsem.at[c],
            device_id={"tensor": other}, device_id_type=MESH,
        )

    @pl.loop(0, nc)
    def _(c):
        down_copy(c).wait()
        cross_out[c] = jnp.dot(hidden[...], w_down[c], preferred_element_type=F32)
        cross_copy(c).start()

    def out_copy(g, d, source):
        to = peer(d)
        row = to if source else me
        return pltpu.make_async_remote_copy(
            src_ref=osnd[g].at[to], dst_ref=orecv[g].at[row],
            send_sem=out_ssem.at[g, d], recv_sem=out_rsem.at[g, row],
            device_id={"expert": to}, device_id_type=MESH,
        )

    first = 0
    for g, count in enumerate(groups):
        for c in range(count):
            at = nc + first + c
            down_copy(at).wait()
            result = jnp.dot(hidden[...], w_down[at], preferred_element_type=F32)
            cross_copy(first + c).wait_recv()
            part32[:, c * chunk : (c + 1) * chunk] = result + cross_in[first + c]

        def pack(i, g=g, count=count):
            osnd[g][i] = part32[pl.ds(i * CAP, CAP), : count * chunk].astype(BF16)

        each(n, pack)

        @pl.loop(1, n)
        def _(d, g=g):
            out_copy(g, d, False).start()

        orecv[g][me] = osnd[g][me]
        first += count

    lanes = lax.broadcasted_iota(jnp.int32, (tok_rows, 1), 0)
    key = jnp.zeros((tok_rows, 1), jnp.int32)
    for i in range(tok_rows):
        key = jnp.where(lanes == i, keys[i], key)
    first = 0
    for g, count in enumerate(groups):

        @pl.loop(1, n)
        def _(d, g=g):
            out_copy(g, d, True).wait_recv()

        width = count * chunk
        for e in range(NE):
            if per <= 8:
                rows = orecv[g][e * per].astype(F32)
                for j in range(1, per):
                    rows = rows + orecv[g][e * per + j].astype(F32)
                summed[e * CAP : (e + 1) * CAP, :width] = rows
            else:
                summed[e * CAP : (e + 1) * CAP, :width] = jnp.zeros((CAP, width), F32)

                @pl.loop(0, per)
                def _(j, g=g, e=e, width=width):
                    summed[e * CAP : (e + 1) * CAP, :width] += orecv[g][e * per + j].astype(F32)

        mine = jnp.zeros((tok_rows, width), F32)
        for r in range(NE * CAP):
            mine = mine + jnp.where(key == r, 1.0, 0.0).astype(F32) * summed[r : r + 1, :width]
        out_ref[:, first * chunk : first * chunk + width] = mine
        first += count

    flat_copy.wait_send()

    @pl.loop(1, n)
    def _(d):
        send_copy(d).wait_send()

    @pl.loop(0, nc)
    def _(c):
        cross_copy(c).wait_send()

    for g in range(len(groups)):

        @pl.loop(1, n)
        def _(d, g=g):
            out_copy(g, d, False).wait_send()


def local(tokens, expert_ids, route_scale, gate_weight, up_weight, down_weight):
    n = lax.axis_size("expert")
    tok_rows, half = tokens.shape
    width = gate_weight.shape[2]
    rows = n * CAP
    chunk = chunk_of(half)
    nc = half // chunk
    groups = groups_of(nc)
    sizes = [g * chunk for g in groups]
    if len(sizes) == 1:
        sizes = sizes + sizes
    dma = pltpu.SemaphoreType.DMA
    vmem = pl.BlockSpec(memory_space=pltpu.VMEM)
    smem = pl.BlockSpec(memory_space=pltpu.SMEM)
    hbm = pl.BlockSpec(memory_space=pl.ANY)
    summed = pl.pallas_call(
        functools.partial(kernel, n),
        out_shape=jax.ShapeDtypeStruct((tok_rows, half), F32),
        in_specs=[smem, vmem, hbm, hbm, hbm],
        out_specs=vmem,
        scratch_shapes=[
            pltpu.VMEM((2 * nc, chunk, width), BF16),
            pltpu.VMEM((2 * nc, chunk, width), BF16),
            pltpu.VMEM((2 * nc, width, chunk), BF16),
            pltpu.VMEM((NE * CAP, half), F32),
            pltpu.VMEM((NE, CAP, half), BF16),
            pltpu.VMEM((n, CAP, half), BF16),
            pltpu.VMEM((rows, half), F32),
            pltpu.VMEM((nc, rows, chunk), BF16),
            pltpu.VMEM((nc, rows, chunk), BF16),
            pltpu.VMEM((rows, width), F32),
            pltpu.VMEM((rows, width), F32),
            pltpu.VMEM((rows, width), BF16),
            pltpu.VMEM((nc, rows, chunk), F32),
            pltpu.VMEM((nc, rows, chunk), F32),
            pltpu.VMEM((rows, sizes[0]), F32),
            pltpu.VMEM((NE * CAP, sizes[0]), F32),
            pltpu.VMEM((n, CAP, sizes[0]), BF16),
            pltpu.VMEM((n, CAP, sizes[0]), BF16),
            pltpu.VMEM((n, CAP, sizes[1]), BF16),
            pltpu.VMEM((n, CAP, sizes[1]), BF16),
            dma((2 * nc,)),
            dma((2 * nc,)),
            dma((2 * nc,)),
            dma((n,)),
            dma((n,)),
            dma((2,)),
            dma((nc,)),
            dma((nc,)),
            dma((2, n)),
            dma((2, n)),
        ],
        compiler_params=pltpu.CompilerParams(
            collective_id=0, has_side_effects=True, vmem_limit_bytes=66_900_000
        ),
        cost_estimate=pl.CostEstimate(
            flops=6 * rows * 2 * half * width, bytes_accessed=12 * half * width, transcendentals=rows * width
        ),
    )(expert_ids.reshape(tok_rows), tokens, gate_weight, up_weight, down_weight)
    return (summed * route_scale[:, None]).astype(BF16)


def solution(mesh):
    in_specs = (
        P(("group", "expert"), "tensor"),
        P(("group", "expert"), None),
        P(("group", "expert")),
        P("expert", None, "tensor"),
        P("expert", None, "tensor"),
        P("expert", "tensor", None),
    )
    out_specs = P(("group", "expert"), "tensor")
    return jax.shard_map(local, mesh=mesh, in_specs=in_specs, out_specs=out_specs, check_vma=False)
```
